32 devices in a mesh: grp: 2 (over y), wide: 4 (over z), narrow: 4 (over x, core).
Axes of the slice: x: 2, y: 2, z: 4, core: 2. Of those that a mesh axis runs over, the one named last changes fastest.
Arguments:
- hidden_in: bfloat16 [384, 16384], P(('grp', 'wide'), 'narrow'), parts along dimension 0, may hold values from -240 to 240
- norm_gain: float32 [16384], P('narrow'), may hold values from 0.1 to 1.9
- query_weight: bfloat16 [16384, 16384], P('narrow', 'wide'), may hold values from -0.046875 to 0.046875
- key_weight: bfloat16 [16384, 1024], P('narrow', 'wide'), may hold values from -0.046875 to 0.046875
- value_weight: bfloat16 [16384, 1024], P('narrow', 'wide'), may hold values from -0.046875 to 0.046875
- positions: int32 [384], P(('grp', 'narrow')), parts along dimension 0, may hold values from 0 to 8191
Outputs:
- queries: bfloat16 [384, 16384], P(('grp', 'narrow'), 'wide'), parts along dimension 0
- keys_new: bfloat16 [384, 1024], P(('grp', 'narrow'), 'wide'), parts along dimension 0
- values_new: bfloat16 [384, 1024], P(('grp', 'narrow'), 'wide'), parts along dimension 0
The draws below stay inside these ranges and needn't reach their ends.
There are 2 independent parts, one for each index of `grp`. The reference program is written for one: setup_inputs(seed, part) draws one part's arguments, and reference() takes and returns one part's arrays. A program takes and returns all parts, laid end to end along the dimension named above; an argument that names none is the same for every part. Nothing has to cross between parts.
All inputs are finite; a program needn't handle non-finite values.
Results may differ from the reference program's by a relative error of at most 0.005.
Values may be sent and summed in bfloat16 or wider, within the bound.
A program may use at most 128 MiB of HBM per device.

```python
import math
import jax
import jax.numpy as jnp
from jax import lax

D = 16384
HEADS = 128
KV_HEADS = 8
HEAD_DIM = 128
ROWS = 192


def draw_hidden_in(key, part):
    key = jax.random.fold_in(key, 11)
    key_base, key_rows, key_cols = jax.random.split(key, 3)
    column_pos = jnp.arange(D, dtype=jnp.float32) / D
    base = jnp.clip(jax.random.normal(key_base, (ROWS, D), jnp.float32), -4.0, 4.0)
    row_scale = jnp.exp(jax.random.uniform(key_rows, (ROWS, 1), jnp.float32, 0.0, math.log(10.0)))
    col_scale = jnp.exp(column_pos * math.log(3.0)) * jnp.exp(jax.random.uniform(key_cols, (D,), jnp.float32, 0.0, math.log(2.0)))
    return (base * row_scale * col_scale[None, :]).astype(jnp.bfloat16)


def set_ends(drawn, rng, least, top_value):
    place = [jax.random.randint(jax.random.fold_in(rng, axis), (), 0, length) for axis, length in enumerate(drawn.shape)]
    widest = drawn.shape.index(max(drawn.shape))
    next_to = place[:widest] + [(place[widest] + 1) % drawn.shape[widest]] + place[widest + 1:]
    return drawn.at[tuple(place)].set(least).at[tuple(next_to)].set(top_value)


def block_scale(stream_key, shape, pieces, smallest, high):
    loudness = 1.0
    for axis_at, parts in pieces:
        heights = jax.random.uniform(jax.random.fold_in(jax.random.fold_in(stream_key, 6), axis_at), (parts,), jnp.float32, smallest / len(pieces), high / len(pieces))
        loudness = loudness * jnp.repeat(jnp.exp(heights), shape[axis_at] // parts).reshape((-1,) + (1,) * (len(shape) - 1 - axis_at))
    return loudness


def scatter_about(rng, shape, deviation, most, pieces=(), held_as=jnp.bfloat16):
    result = deviation * jax.random.normal(rng, shape, jnp.float32)
    if pieces:
        result = result * block_scale(rng, shape, pieces, -0.22, 0.18)
    return jnp.clip(result, -most, most).astype(held_as)


def setup_inputs(seed: int = 0, part: int = 0) -> dict:
    arg_keys = jax.random.split(jax.random.key(seed), 7)
    part_splits = jax.random.split(jax.random.fold_in(arg_keys[6], part), 7)
    return {
        "hidden_in": draw_hidden_in(jax.random.fold_in(jax.random.fold_in(arg_keys[6], part), 71), part),
        "norm_gain": jnp.clip(1.0 + 0.18 * jax.random.normal(arg_keys[1], (D,), jnp.float32), 0.1, 1.9),
        "query_weight": scatter_about(arg_keys[2], (D, HEADS * HEAD_DIM), D ** -0.5, 0.046875, ((0, 4), (1, 4))),
        "key_weight": scatter_about(arg_keys[3], (D, KV_HEADS * HEAD_DIM), D ** -0.5, 0.046875, ((0, 4), (1, 4))),
        "value_weight": scatter_about(arg_keys[4], (D, KV_HEADS * HEAD_DIM), D ** -0.5, 0.046875, ((0, 4), (1, 4))),
        "positions": set_ends(jax.random.randint(part_splits[5], (ROWS,), 0, 8192), jax.random.fold_in(part_splits[5], 1), 0, 8191).astype(jnp.int32),
    }


def frequency(pair_index, head_dim):
    base = jnp.float32(500000.0) ** (-2.0 * pair_index / jnp.float32(head_dim))
    wavelen = 2.0 * math.pi / base
    smooth = (8192.0 / wavelen - 1.0) / 3.0
    middle = (1.0 - smooth) * base / 8.0 + smooth * base
    return jnp.where(wavelen < 2048.0, base, jnp.where(wavelen > 8192.0, base / 8.0, middle))

def rotate(block, positions, offset):
    count, width = block.shape
    pairs = block.reshape(count, width // 2, 2)
    first = pairs[:, :, 0]
    second = pairs[:, :, 1]
    columns = offset + 2 * jnp.arange(width // 2, dtype=jnp.int32)
    pair_index = (columns % HEAD_DIM // 2).astype(jnp.float32)
    angle = positions.astype(jnp.float32)[:, None] * frequency(pair_index, HEAD_DIM)[None, :]
    cosine = jnp.cos(angle)
    sine = jnp.sin(angle)
    turned = jnp.stack([first * cosine - second * sine, first * sine + second * cosine], axis=-1)
    return turned.reshape(count, width)

def reference(hidden_in, norm_gain, query_weight, key_weight, value_weight, positions):
    raw = hidden_in.astype(jnp.float32)
    scaled = (raw * norm_gain[None, :]).astype(jnp.bfloat16)
    squares = lax.optimization_barrier(jnp.sum(raw * raw, axis=1))
    inverse = lax.rsqrt(squares / D + 1e-05)
    proj_q = jnp.dot(scaled, query_weight, preferred_element_type=jnp.float32)
    proj_k = jnp.dot(scaled, key_weight, preferred_element_type=jnp.float32)
    proj_v = jnp.dot(scaled, value_weight, preferred_element_type=jnp.float32)
    queries = rotate(proj_q * inverse[:, None], positions, 0).astype(jnp.bfloat16)
    keys_new = rotate(proj_k * inverse[:, None], positions, 0).astype(jnp.bfloat16)
    values_new = (proj_v * inverse[:, None]).astype(jnp.bfloat16)
    return (queries, keys_new, values_new)
```

```python
import functools
import math

import jax
import jax.numpy as jnp
from jax import lax
from jax.experimental import pallas as pl
from jax.experimental.pallas import tpu as pltpu
from jax.sharding import PartitionSpec as P

D = 16384
HEAD_DIM = 128
LANES = 128
MESH_ID = pl.DeviceIdType.MESH


def frequency(pair_index, head_dim):
    base = jnp.float32(500000.0) ** (-2.0 * pair_index / jnp.float32(head_dim))
    wavelen = 2.0 * math.pi / base
    smooth = (8192.0 / wavelen - 1.0) / 3.0
    middle = (1.0 - smooth) * base / 8.0 + smooth * base
    return jnp.where(wavelen < 2048.0, base, jnp.where(wavelen > 8192.0, base / 8.0, middle))


def turn(u, cosine, sine):
    lane = lax.broadcasted_iota(jnp.int32, u.shape, 1)
    other = jnp.where(lane % 2 == 0, pltpu.roll(u, LANES - 1, 1), pltpu.roll(u, 1, 1))
    return u * cosine + other * sine


def kernel(n, parts_kv, width, mid, hid, gain, cos, sin, kcos, ksin, wq, *rest):
    wkv = rest[:parts_kv]
    (out_q, out_k, out_v, raw, scaled, wq_v, wkv_v, stage_q, stage_s, got_q, got_s, own_q, own_s,
     up_sem, down_sem, in_sem, wq_sem, wkv_sem, sq_sem, ss_sem, rq_sem, rs_sem) = rest[parts_kv:]
    me = lax.axis_index("wide")
    nar = lax.axis_index("narrow")
    depth = hid.shape[1]
    chunks = wq_v.shape[0]
    kv = wkv_v.shape[1]
    key_cols = kv // 2

    def q_weight(c):
        return pltpu.make_async_copy(wq.at[:, pl.ds(pl.multiple_of(c * width, width), width)], wq_v.at[c], wq_sem.at[c])

    def kv_weight(i):
        w = kv // parts_kv
        return pltpu.make_async_copy(wkv[i], wkv_v.at[:, pl.ds(i * w, w)], wkv_sem.at[i])

    def up(blk):
        return pltpu.make_async_remote_copy(
            src_ref=raw.at[blk], dst_ref=raw.at[blk], send_sem=up_sem.at[blk], recv_sem=in_sem.at[blk],
            device_id={"wide": lax.rem(me + 1, n)}, device_id_type=MESH_ID)

    def down(blk):
        return pltpu.make_async_remote_copy(
            src_ref=raw.at[blk], dst_ref=raw.at[blk], send_sem=down_sem.at[blk], recv_sem=in_sem.at[blk],
            device_id={"wide": lax.rem(me + n - 1, n)}, device_id_type=MESH_ID)

    def send_q(blk, c):
        return pltpu.make_async_remote_copy(
            src_ref=stage_q.at[blk, c], dst_ref=got_q.at[nar, c], send_sem=sq_sem.at[blk, c],
            recv_sem=rq_sem.at[nar, c], device_id={"narrow": blk}, device_id_type=MESH_ID)

    def send_s(blk):
        return pltpu.make_async_remote_copy(
            src_ref=stage_s.at[blk], dst_ref=got_s.at[nar], send_sem=ss_sem.at[blk],
            recv_sem=rs_sem.at[nar], device_id={"narrow": blk}, device_id_type=MESH_ID)

    for i in range(parts_kv):
        kv_weight(i).start()

    @pl.loop(0, chunks)
    def _(c):
        q_weight(c).start()

    raw[me] = hid[...]
    barrier = pltpu.get_barrier_semaphore()

    @pl.when(me < n - 1)
    def _():
        pl.semaphore_signal(barrier, inc=1, device_id={"wide": lax.rem(me + 1, n)}, device_id_type=MESH_ID)

    @pl.when(me > 0)
    def _():
        pl.semaphore_signal(barrier, inc=1, device_id={"wide": lax.rem(me + n - 1, n)}, device_id_type=MESH_ID)

    for i in range(1, n):
        pl.semaphore_signal(barrier, inc=1, device_id={"narrow": lax.rem(nar + i, n)}, device_id_type=MESH_ID)
    edge = jnp.where(me > 0, 1, 0) + jnp.where(me < n - 1, 1, 0)
    pl.semaphore_wait(barrier, n - 1 + edge)

    @pl.when(me < n - 1)
    def _():
        up(me).start()

    @pl.when(me > 0)
    def _():
        down(me).start()

    def forward(d):
        low = me - d
        high = me + d

        @pl.when((low >= 0) & (me < n - 1))
        def _():
            up(low).wait_recv()
            up(low).start()

        @pl.when((high < n) & (me > 0))
        def _():
            down(high).wait_recv()
            down(high).start()

    @pl.loop(0, 2 * n - 1)
    def _(j):
        d = (j + 1) // 2
        minus = lax.rem(j, 2) == 1
        blk = jnp.where(minus, me - d, me + d)
        valid = (blk >= 0) & (blk < n)
        lead = minus | (j == 0) | (me - d < 0)

        @pl.when(valid)
        def _():
            last_here = jnp.where(minus, me == n - 1, me == 0)

            @pl.when((j > 0) & last_here)
            def _():
                up(blk).wait_recv()

            def prep(k, sq):
                for t in range(4):
                    at = pl.ds(pl.multiple_of(k * (4 * LANES) + t * LANES, LANES), LANES)
                    x = raw[blk, :, at].astype(jnp.float32)
                    scaled[:, at] = (x * gain[:, at]).astype(jnp.bfloat16)
                    sq = sq + x * x
                return sq

            rows = hid.shape[0]
            sq = lax.fori_loop(0, depth // (4 * LANES), prep, jnp.zeros((rows, LANES), jnp.float32))

            @pl.when(j == 0)
            def _():
                for i in range(parts_kv):
                    kv_weight(i).wait()

            part = jnp.dot(scaled[...], wkv_v[...], preferred_element_type=jnp.float32)
            mine = blk == nar

            @pl.when(mine)
            def _():
                own_s[:, :kv] = part
                own_s[:, kv:] = sq

            @pl.when(jnp.logical_not(mine))
            def _():
                stage_s[blk, :, :kv] = part.astype(jnp.bfloat16)
                coarse = sq.astype(jnp.bfloat16)
                stage_s[blk, :, kv:kv + LANES] = coarse
                stage_s[blk, :, kv + LANES:] = (sq - coarse.astype(jnp.float32)).astype(jnp.bfloat16)
                send_s(blk).start()

            @pl.loop(0, chunks)
            def _(c):
                @pl.when(j == 0)
                def _():
                    q_weight(c).wait()

                piece = jnp.dot(scaled[...], wq_v[c], preferred_element_type=jnp.float32)

                @pl.when(mine)
                def _():
                    own_q[c] = piece

                @pl.when(jnp.logical_not(mine))
                def _():
                    stage_q[blk, c] = piece.astype(jnp.bfloat16)
                    send_q(blk, c).start()

                @pl.when(lead & (c == mid))
                def _():
                    forward(d + 1)

    def recv_s(p):
        return pltpu.make_async_remote_copy(
            src_ref=stage_s.at[p], dst_ref=got_s.at[p], send_sem=ss_sem.at[p], recv_sem=rs_sem.at[p],
            device_id={"narrow": p}, device_id_type=MESH_ID)

    def recv_q(p, c):
        return pltpu.make_async_remote_copy(
            src_ref=stage_q.at[p, c], dst_ref=got_q.at[p, c], send_sem=sq_sem.at[p, c], recv_sem=rq_sem.at[p, c],
            device_id={"narrow": p}, device_id_type=MESH_ID)

    for i in range(1, n):
        p = lax.rem(nar + i, n)
        recv_s(p).wait_recv()
        block = got_s[p].astype(jnp.float32)
        own_s[:, :kv] += block[:, :kv]
        own_s[:, kv:] += block[:, kv:kv + LANES] + block[:, kv + LANES:]
    squares = jnp.sum(own_s[:, kv:], axis=1, keepdims=True)
    inverse = lax.rsqrt(squares / D + 1e-05)
    made = []
    for t in range(kv // LANES):
        at = slice(t * LANES, (t + 1) * LANES)
        made.append(turn(own_s[:, at] * inverse, kcos[:, at], ksin[:, at]))
    joint = jnp.concatenate(made, axis=1) if len(made) > 1 else made[0]
    out_k[...] = joint[:, :key_cols].astype(jnp.bfloat16)
    out_v[...] = joint[:, key_cols:].astype(jnp.bfloat16)

    @pl.loop(0, chunks)
    def _(c):
        for i in range(1, n):
            recv_q(lax.rem(nar + i, n), c).wait_recv()
        for t in range(width // LANES):
            at = pl.ds(t * LANES, LANES)
            u = own_q[c, :, at]
            for i in range(1, n):
                u = u + got_q[lax.rem(nar + i, n), c, :, at].astype(jnp.float32)
            turned = turn(u * inverse, cos[...], sin[...])
            out_q[:, pl.ds(pl.multiple_of(c * width + t * LANES, LANES), LANES)] = turned.astype(jnp.bfloat16)

    @pl.loop(0, n)
    def _(b):
        @pl.when((b <= me) & (me < n - 1))
        def _():
            up(b).wait_send()

        @pl.when((b >= me) & (me > 0))
        def _():
            down(b).wait_send()

    for i in range(1, n):
        b = lax.rem(nar + i, n)
        send_s(b).wait_send()

        @pl.loop(0, chunks)
        def _(c):
            send_q(b, c).wait_send()


def shards(n, hidden_in, norm_gain, query_weight, key_weight, value_weight, positions):
    rows, depth = hidden_in.shape
    query_cols = query_weight.shape[1]
    key_cols = key_weight.shape[1]
    kv = 2 * key_cols
    width = 512
    chunks = query_cols // width
    lanes = jnp.arange(HEAD_DIM, dtype=jnp.int32)
    angle = positions.astype(jnp.float32)[:, None] * frequency((lanes // 2).astype(jnp.float32), HEAD_DIM)[None, :]
    cosine = jnp.cos(angle)
    sine = jnp.where(lanes % 2 == 0, -1.0, 1.0)[None, :] * jnp.sin(angle)
    if key_cols % HEAD_DIM == 0:
        copies = key_cols // HEAD_DIM
        key_cos, key_sin = jnp.tile(cosine, (1, copies)), jnp.tile(sine, (1, copies))
        weights = (key_weight, value_weight)
    else:
        start = lax.axis_index("wide") * key_cols % HEAD_DIM
        key_cos = lax.dynamic_slice_in_dim(cosine, start, key_cols, 1)
        key_sin = lax.dynamic_slice_in_dim(sine, start, key_cols, 1)
        weights = (jnp.concatenate([key_weight, value_weight], axis=1),)
    key_cos = jnp.concatenate([key_cos, jnp.ones_like(key_cos)], axis=1)
    key_sin = jnp.concatenate([key_sin, jnp.zeros_like(key_sin)], axis=1)
    vmem = pl.BlockSpec(memory_space=pltpu.VMEM)
    hbm = pl.BlockSpec(memory_space=pl.ANY)
    bf, f32 = jnp.bfloat16, jnp.float32
    dma = pltpu.SemaphoreType.DMA
    return pl.pallas_call(
        functools.partial(kernel, n, len(weights), width, chunks * 3 // 4),
        out_shape=(
            jax.ShapeDtypeStruct((rows, query_cols), bf),
            jax.ShapeDtypeStruct((rows, key_cols), bf),
            jax.ShapeDtypeStruct((rows, key_cols), bf),
        ),
        in_specs=[vmem] * 6 + [hbm] * (1 + len(weights)),
        out_specs=(vmem, vmem, vmem),
        scratch_shapes=[
            pltpu.VMEM((n, rows, depth), bf),
            pltpu.VMEM((rows, depth), bf),
            pltpu.VMEM((chunks, depth, width), bf),
            pltpu.VMEM((depth, kv), bf),
            pltpu.VMEM((n, chunks, rows, width), bf),
            pltpu.VMEM((n, rows, kv + 2 * LANES), bf),
            pltpu.VMEM((n, chunks, rows, width), bf),
            pltpu.VMEM((n, rows, kv + 2 * LANES), bf),
            pltpu.VMEM((chunks, rows, width), f32),
            pltpu.VMEM((rows, kv + LANES), f32),
            dma((n,)), dma((n,)), dma((n,)),
            dma((chunks,)), dma((len(weights),)),
            dma((n, chunks)), dma((n,)),
            dma((n, chunks)), dma((n,)),
        ],
        compiler_params=pltpu.CompilerParams(
            collective_id=0, has_side_effects=True, vmem_limit_bytes=58 * 1024 * 1024),
        cost_estimate=pl.CostEstimate(
            flops=2 * n * rows * depth * (query_cols + kv),
            bytes_accessed=2 * depth * (query_cols + kv), transcendentals=0),
    )(hidden_in, norm_gain[None, :], cosine, sine, key_cos, key_sin, query_weight, *weights)


def solution(mesh):
    n = mesh.shape["narrow"]
    assert mesh.shape["wide"] == n
    return jax.shard_map(
        functools.partial(shards, n),
        mesh=mesh,
        in_specs=(
            P(("grp", "wide"), "narrow"),
            P("narrow"),
            P("narrow", "wide"),
            P("narrow", "wide"),
            P("narrow", "wide"),
            P(("grp", "narrow")),
        ),
        out_specs=(
            P(("grp", "narrow"), "wide"),
            P(("grp", "narrow"), "wide"),
            P(("grp", "narrow"), "wide"),
        ),
        check_vma=False,
    )
```

```python
import functools
import math

import jax
import jax.numpy as jnp
from jax import lax
from jax.experimental import pallas as pl
from jax.experimental.pallas import tpu as pltpu
from jax.sharding import PartitionSpec as P

D = 16384
HEAD_DIM = 128
LANES = 128
MESH_ID = pl.DeviceIdType.MESH


def frequency(pair_index, head_dim):
    base = jnp.float32(500000.0) ** (-2.0 * pair_index / jnp.float32(head_dim))
    wavelen = 2.0 * math.pi / base
    smooth = (8192.0 / wavelen - 1.0) / 3.0
    middle = (1.0 - smooth) * base / 8.0 + smooth * base
    return jnp.where(wavelen < 2048.0, base, jnp.where(wavelen > 8192.0, base / 8.0, middle))


def turn(u, cosine, sine):
    lane = lax.broadcasted_iota(jnp.int32, u.shape, 1)
    other = jnp.where(lane % 2 == 0, pltpu.roll(u, LANES - 1, 1), pltpu.roll(u, 1, 1))
    return u * cosine + other * sine


def kernel(n, parts_kv, width, pieces, points, aligned, hid, gain, cos, sin, *rest):
    tables = rest[:0 if aligned else 2]
    wq, rest = rest[len(tables)], rest[len(tables) + 1:]
    wkv = rest[:parts_kv]
    (out_q, out_k, out_v, raw, scaled, wq_v, wkv_v, stage_q, stage_s, got_q, got_s, own_q, own_s,
     up_sem, down_sem, in_sem, wq_sem, wkv_sem, sq_sem, ss_sem, rq_sem, rs_sem) = rest[parts_kv:]
    me = lax.axis_index("wide")
    nar = lax.axis_index("narrow")
    depth = hid.shape[1]
    chunks = wq_v.shape[0]
    kv = wkv_v.shape[1]
    key_cols = kv // 2

    def q_weight(c):
        return pltpu.make_async_copy(wq.at[:, pl.ds(pl.multiple_of(c * width, width), width)], wq_v.at[c], wq_sem.at[c])

    def kv_weight(i):
        w = kv // parts_kv
        return pltpu.make_async_copy(wkv[i], wkv_v.at[:, pl.ds(i * w, w)], wkv_sem.at[i])

    def up(blk, h):
        return pltpu.make_async_remote_copy(
            src_ref=raw.at[blk, h], dst_ref=raw.at[blk, h], send_sem=up_sem.at[blk, h], recv_sem=in_sem.at[blk, h],
            device_id={"wide": lax.rem(me + 1, n)}, device_id_type=MESH_ID)

    def down(blk, h):
        return pltpu.make_async_remote_copy(
            src_ref=raw.at[blk, h], dst_ref=raw.at[blk, h], send_sem=down_sem.at[blk, h], recv_sem=in_sem.at[blk, h],
            device_id={"wide": lax.rem(me + n - 1, n)}, device_id_type=MESH_ID)

    def send_q(blk, c):
        return pltpu.make_async_remote_copy(
            src_ref=stage_q.at[blk, c], dst_ref=got_q.at[nar, c], send_sem=sq_sem.at[blk, c],
            recv_sem=rq_sem.at[nar, c], device_id={"narrow": blk}, device_id_type=MESH_ID)

    def send_s(blk):
        return pltpu.make_async_remote_copy(
            src_ref=stage_s.at[blk], dst_ref=got_s.at[nar], send_sem=ss_sem.at[blk],
            recv_sem=rs_sem.at[nar], device_id={"narrow": blk}, device_id_type=MESH_ID)

    for i in range(parts_kv):
        kv_weight(i).start()

    @pl.loop(0, chunks)
    def _(c):
        q_weight(c).start()

    cut = depth // pieces
    for h in range(pieces):
        raw[me, h] = hid[:, h * cut:(h + 1) * cut]
    barrier = pltpu.get_barrier_semaphore()

    @pl.when(me < n - 1)
    def _():
        pl.semaphore_signal(barrier, inc=1, device_id={"wide": lax.rem(me + 1, n)}, device_id_type=MESH_ID)

    @pl.when(me > 0)
    def _():
        pl.semaphore_signal(barrier, inc=1, device_id={"wide": lax.rem(me + n - 1, n)}, device_id_type=MESH_ID)

    for i in range(1, n):
        pl.semaphore_signal(barrier, inc=1, device_id={"narrow": lax.rem(nar + i, n)}, device_id_type=MESH_ID)
    edge = jnp.where(me > 0, 1, 0) + jnp.where(me < n - 1, 1, 0)
    pl.semaphore_wait(barrier, n - 1 + edge)

    @pl.when(me < n - 1)
    def _():
        for h in range(pieces):
            up(me, h).start()

    @pl.when(me > 0)
    def _():
        for h in range(pieces):
            down(me, h).start()

    def forward(d, h):
        low = me - d
        high = me + d

        @pl.when((low >= 0) & (me < n - 1))
        def _():
            up(low, h).wait_recv()
            up(low, h).start()

        @pl.when((high < n) & (me > 0))
        def _():
            down(high, h).wait_recv()
            down(high, h).start()

    @pl.loop(0, 2 * n - 1)
    def _(j):
        d = (j + 1) // 2
        minus = lax.rem(j, 2) == 1
        blk = jnp.where(minus, me - d, me + d)
        valid = (blk >= 0) & (blk < n)
        lead = minus | (j == 0) | (me - d < 0)

        @pl.when(valid)
        def _():
            last_here = jnp.where(minus, me == n - 1, me == 0)

            @pl.when((j > 0) & last_here)
            def _():
                for h in range(pieces):
                    up(blk, h).wait_recv()

            def prep(k, sq, h):
                for t in range(min(4, cut // LANES)):
                    at = pl.ds(pl.multiple_of(k * (4 * LANES) + t * LANES, LANES), LANES)
                    x = raw[blk, h, :, at].astype(jnp.float32)
                    to = pl.ds(pl.multiple_of(h * cut + k * (4 * LANES) + t * LANES, LANES), LANES)
                    scaled[:, to] = (x * gain[:, to]).astype(jnp.bfloat16)
                    sq = sq + x * x
                return sq

            rows = hid.shape[0]
            sq = jnp.zeros((rows, LANES), jnp.float32)
            for h in range(pieces):
                sq = lax.fori_loop(0, max(1, cut // (4 * LANES)), functools.partial(prep, h=h), sq)

            @pl.when(j == 0)
            def _():
                for i in range(parts_kv):
                    kv_weight(i).wait()

            part = jnp.dot(scaled[...], wkv_v[...], preferred_element_type=jnp.float32)
            mine = blk == nar

            @pl.when(mine)
            def _():
                own_s[:, :kv] = part
                own_s[:, kv:] = sq

            @pl.when(jnp.logical_not(mine))
            def _():
                stage_s[blk, :, :kv] = part.astype(jnp.bfloat16)
                coarse = sq.astype(jnp.bfloat16)
                stage_s[blk, :, kv:kv + LANES] = coarse
                stage_s[blk, :, kv + LANES:] = (sq - coarse.astype(jnp.float32)).astype(jnp.bfloat16)
                send_s(blk).start()

            @pl.loop(0, chunks)
            def _(c):
                @pl.when(j == 0)
                def _():
                    q_weight(c).wait()

                piece = jnp.dot(scaled[...], wq_v[c], preferred_element_type=jnp.float32)

                @pl.when(mine)
                def _():
                    own_q[c] = piece

                @pl.when(jnp.logical_not(mine))
                def _():
                    stage_q[blk, c] = piece.astype(jnp.bfloat16)
                    send_q(blk, c).start()

                for h in range(pieces):
                    @pl.when(lead & (c == jnp.where(j == 0, points[0][h], points[1][h])))
                    def _():
                        forward(d + 1, h)

    def recv_s(p):
        return pltpu.make_async_remote_copy(
            src_ref=stage_s.at[p], dst_ref=got_s.at[p], send_sem=ss_sem.at[p], recv_sem=rs_sem.at[p],
            device_id={"narrow": p}, device_id_type=MESH_ID)

    def recv_q(p, c):
        return pltpu.make_async_remote_copy(
            src_ref=stage_q.at[p, c], dst_ref=got_q.at[p, c], send_sem=sq_sem.at[p, c], recv_sem=rq_sem.at[p, c],
            device_id={"narrow": p}, device_id_type=MESH_ID)

    for i in range(1, n):
        p = lax.rem(nar + i, n)
        recv_s(p).wait_recv()
        block = got_s[p].astype(jnp.float32)
        own_s[:, :kv] += block[:, :kv]
        own_s[:, kv:] += block[:, kv:kv + LANES] + block[:, kv + LANES:]
    squares = jnp.sum(own_s[:, kv:], axis=1, keepdims=True)
    inverse = lax.rsqrt(squares / D + 1e-05)
    made = []
    for t in range(kv // LANES):
        at = slice(t * LANES, (t + 1) * LANES)
        u = own_s[:, at] * inverse
        if not aligned:
            u = turn(u, tables[0][:, at], tables[1][:, at])
        elif t * LANES < key_cols:
            u = turn(u, cos[...], sin[...])
        made.append(u)
    joint = jnp.concatenate(made, axis=1) if len(made) > 1 else made[0]
    out_k[...] = joint[:, :key_cols].astype(jnp.bfloat16)
    out_v[...] = joint[:, key_cols:].astype(jnp.bfloat16)

    @pl.loop(0, chunks)
    def _(c):
        for i in range(1, n):
            recv_q(lax.rem(nar + i, n), c).wait_recv()
        for t in range(width // LANES):
            at = pl.ds(t * LANES, LANES)
            u = own_q[c, :, at]
            for i in range(1, n):
                u = u + got_q[lax.rem(nar + i, n), c, :, at].astype(jnp.float32)
            turned = turn(u * inverse, cos[...], sin[...])
            out_q[:, pl.ds(pl.multiple_of(c * width + t * LANES, LANES), LANES)] = turned.astype(jnp.bfloat16)

    @pl.loop(0, n)
    def _(b):
        @pl.when((b <= me) & (me < n - 1))
        def _():
            for h in range(pieces):
                up(b, h).wait_send()

        @pl.when((b >= me) & (me > 0))
        def _():
            for h in range(pieces):
                down(b, h).wait_send()

    for i in range(1, n):
        b = lax.rem(nar + i, n)
        send_s(b).wait_send()

        @pl.loop(0, chunks)
        def _(c):
            send_q(b, c).wait_send()


def hand_over(*refs):
    for i in range(3):
        refs[3 + i][...] = refs[i][...]


def shards(n, hidden_in, norm_gain, query_weight, key_weight, value_weight, positions):
    rows, depth = hidden_in.shape
    query_cols = query_weight.shape[1]
    key_cols = key_weight.shape[1]
    kv = 2 * key_cols
    width = 512
    chunks = query_cols // width
    lanes = jnp.arange(HEAD_DIM, dtype=jnp.int32)
    angle = positions.astype(jnp.float32)[:, None] * frequency((lanes // 2).astype(jnp.float32), HEAD_DIM)[None, :]
    cosine = jnp.cos(angle)
    sine = jnp.where(lanes % 2 == 0, -1.0, 1.0)[None, :] * jnp.sin(angle)
    if key_cols % HEAD_DIM == 0:
        tables = ()
        weights = (key_weight, value_weight)
    else:
        start = lax.axis_index("wide") * key_cols % HEAD_DIM
        key_cos = lax.dynamic_slice_in_dim(cosine, start, key_cols, 1)
        key_sin = lax.dynamic_slice_in_dim(sine, start, key_cols, 1)
        weights = (jnp.concatenate([key_weight, value_weight], axis=1),)
        key_cos = jnp.concatenate([key_cos, jnp.ones_like(key_cos)], axis=1)
        key_sin = jnp.concatenate([key_sin, jnp.zeros_like(key_sin)], axis=1)
        tables = (key_cos, key_sin)
    vmem = pl.BlockSpec(memory_space=pltpu.VMEM)
    hbm = pl.BlockSpec(memory_space=pl.ANY)
    bf, f32 = jnp.bfloat16, jnp.float32
    dma = pltpu.SemaphoreType.DMA
    pieces = 2
    points = tuple(tuple(p * chunks // 8 for p in at) for at in ((2, 6), (3, 7)))
    results = pl.pallas_call(
        functools.partial(kernel, n, len(weights), width, pieces, points, not tables),
        out_shape=(
            jax.ShapeDtypeStruct((rows, query_cols), bf),
            jax.ShapeDtypeStruct((rows, key_cols), bf),
            jax.ShapeDtypeStruct((rows, key_cols), bf),
        ),
        in_specs=[vmem] * (4 + len(tables)) + [hbm] * (1 + len(weights)),
        out_specs=(vmem, vmem, vmem),
        scratch_shapes=[
            pltpu.VMEM((n, pieces, rows, depth // pieces), bf),
            pltpu.VMEM((rows, depth), bf),
            pltpu.VMEM((chunks, depth, width), bf),
            pltpu.VMEM((depth, kv), bf),
            pltpu.VMEM((n, chunks, rows, width), bf),
            pltpu.VMEM((n, rows, kv + 2 * LANES), bf),
            pltpu.VMEM((n, chunks, rows, width), bf),
            pltpu.VMEM((n, rows, kv + 2 * LANES), bf),
            pltpu.VMEM((chunks, rows, width), f32),
            pltpu.VMEM((rows, kv + LANES), f32),
            dma((n, pieces)), dma((n, pieces)), dma((n, pieces)),
            dma((chunks,)), dma((len(weights),)),
            dma((n, chunks)), dma((n,)),
            dma((n, chunks)), dma((n,)),
        ],
        compiler_params=pltpu.CompilerParams(
            collective_id=0, has_side_effects=True, vmem_limit_bytes=58 * 1024 * 1024),
        cost_estimate=pl.CostEstimate(
            flops=2 * n * rows * depth * (query_cols + kv),
            bytes_accessed=2 * depth * (query_cols + kv), transcendentals=0),
    )(hidden_in, norm_gain[None, :], cosine, sine, *tables, query_weight, *weights)
    return pl.pallas_call(
        hand_over,
        out_shape=tuple(jax.ShapeDtypeStruct(x.shape, x.dtype) for x in results),
        in_specs=[vmem] * 3,
        out_specs=(vmem,) * 3,
    )(*results)


def solution(mesh):
    n = mesh.shape["narrow"]
    assert mesh.shape["wide"] == n
    return jax.shard_map(
        functools.partial(shards, n),
        mesh=mesh,
        in_specs=(
            P(("grp", "wide"), "narrow"),
            P("narrow"),
            P("narrow", "wide"),
            P("narrow", "wide"),
            P("narrow", "wide"),
            P(("grp", "narrow")),
        ),
        out_specs=(
            P(("grp", "narrow"), "wide"),
            P(("grp", "narrow"), "wide"),
            P(("grp", "narrow"), "wide"),
        ),
        check_vma=False,
    )
```

```python
import functools
import math

import jax
import jax.numpy as jnp
from jax import lax
from jax.experimental import pallas as pl
from jax.experimental.pallas import tpu as pltpu
from jax.sharding import PartitionSpec as P

D = 16384
HEAD_DIM = 128
LANES = 128
MESH_ID = pl.DeviceIdType.MESH


def frequency(pair_index, head_dim):
    base = jnp.float32(500000.0) ** (-2.0 * pair_index / jnp.float32(head_dim))
    wavelen = 2.0 * math.pi / base
    smooth = (8192.0 / wavelen - 1.0) / 3.0
    middle = (1.0 - smooth) * base / 8.0 + smooth * base
    return jnp.where(wavelen < 2048.0, base, jnp.where(wavelen > 8192.0, base / 8.0, middle))


def turn(u, cosine, sine):
    lane = lax.broadcasted_iota(jnp.int32, u.shape, 1)
    other = jnp.where(lane % 2 == 0, pltpu.roll(u, LANES - 1, 1), pltpu.roll(u, 1, 1))
    return u * cosine + other * sine


def kernel(n, parts_kv, width, pieces, points, aligned, hid, gain, cos, sin, *rest):
    tables = rest[:0 if aligned else 2]
    wq, rest = rest[len(tables)], rest[len(tables) + 1:]
    wkv = rest[:parts_kv]
    (out_q, out_k, out_v, raw, scaled, wq_v, wkv_v, stage_q, stage_s, got_q, pair_q, got_s, own_q, own_s,
     up_sem, down_sem, in_sem, wq_sem, wkv_sem, sq_sem, pq_sem, ss_sem, rq_sem, rs_sem) = rest[parts_kv:]
    me = lax.axis_index("wide")
    nar = lax.axis_index("narrow")
    depth = hid.shape[1]
    chunks = wq_v.shape[0]
    kv = wkv_v.shape[1]
    key_cols = kv // 2

    def q_weight(c):
        return pltpu.make_async_copy(wq.at[:, pl.ds(pl.multiple_of(c * width, width), width)], wq_v.at[c], wq_sem.at[c])

    def kv_weight(i):
        w = kv // parts_kv
        return pltpu.make_async_copy(wkv[i], wkv_v.at[:, pl.ds(i * w, w)], wkv_sem.at[i])

    def up(blk, h):
        return pltpu.make_async_remote_copy(
            src_ref=raw.at[blk, h], dst_ref=raw.at[blk, h], send_sem=up_sem.at[blk, h], recv_sem=in_sem.at[blk, h],
            device_id={"wide": lax.rem(me + 1, n)}, device_id_type=MESH_ID)

    def down(blk, h):
        return pltpu.make_async_remote_copy(
            src_ref=raw.at[blk, h], dst_ref=raw.at[blk, h], send_sem=down_sem.at[blk, h], recv_sem=in_sem.at[blk, h],
            device_id={"wide": lax.rem(me + n - 1, n)}, device_id_type=MESH_ID)

    def send_q(blk, c):
        return pltpu.make_async_remote_copy(
            src_ref=stage_q.at[blk, c], dst_ref=got_q.at[nar, c], send_sem=sq_sem.at[blk, c],
            recv_sem=rq_sem.at[nar, c], device_id={"narrow": blk}, device_id_type=MESH_ID)

    core = lax.rem(nar, 2)
    chip = nar // 2
    buddy = nar + 1 - 2 * core

    def swap_q(blk, c):
        return pltpu.make_async_remote_copy(
            src_ref=stage_q.at[blk, c], dst_ref=pair_q.at[blk, c], send_sem=sq_sem.at[blk, c],
            recv_sem=pq_sem.at[blk, c], device_id={"narrow": buddy}, device_id_type=MESH_ID)

    def combine(blk, c):
        swap_q(blk, c).wait_recv()
        both = stage_q[blk, c].astype(jnp.float32) + pair_q[blk, c].astype(jnp.float32)
        stage_q[blk, c] = both.astype(jnp.bfloat16)
        send_q(blk, c).start()

    def send_s(blk):
        return pltpu.make_async_remote_copy(
            src_ref=stage_s.at[blk], dst_ref=got_s.at[nar], send_sem=ss_sem.at[blk],
            recv_sem=rs_sem.at[nar], device_id={"narrow": blk}, device_id_type=MESH_ID)

    for i in range(parts_kv):
        kv_weight(i).start()

    @pl.loop(0, chunks)
    def _(c):
        q_weight(c).start()

    cut = depth // pieces
    for h in range(pieces):
        raw[me, h] = hid[:, h * cut:(h + 1) * cut]
    barrier = pltpu.get_barrier_semaphore()

    @pl.when(me < n - 1)
    def _():
        pl.semaphore_signal(barrier, inc=1, device_id={"wide": lax.rem(me + 1, n)}, device_id_type=MESH_ID)

    @pl.when(me > 0)
    def _():
        pl.semaphore_signal(barrier, inc=1, device_id={"wide": lax.rem(me + n - 1, n)}, device_id_type=MESH_ID)

    for i in range(1, n):
        pl.semaphore_signal(barrier, inc=1, device_id={"narrow": lax.rem(nar + i, n)}, device_id_type=MESH_ID)
    edge = jnp.where(me > 0, 1, 0) + jnp.where(me < n - 1, 1, 0)
    pl.semaphore_wait(barrier, n - 1 + edge)

    @pl.when(me < n - 1)
    def _():
        for h in range(pieces):
            up(me, h).start()

    @pl.when(me > 0)
    def _():
        for h in range(pieces):
            down(me, h).start()

    def forward(d, h):
        low = me - d
        high = me + d

        @pl.when((low >= 0) & (me < n - 1))
        def _():
            up(low, h).wait_recv()
            up(low, h).start()

        @pl.when((high < n) & (me > 0))
        def _():
            down(high, h).wait_recv()
            down(high, h).start()

    @pl.loop(0, 2 * n - 1)
    def _(j):
        d = (j + 1) // 2
        minus = lax.rem(j, 2) == 1
        blk = jnp.where(minus, me - d, me + d)
        valid = (blk >= 0) & (blk < n)
        lead = minus | (j == 0) | (me - d < 0)

        @pl.when(valid)
        def _():
            last_here = jnp.where(minus, me == n - 1, me == 0)

            @pl.when((j > 0) & last_here)
            def _():
                for h in range(pieces):
                    up(blk, h).wait_recv()

            def prep(k, sq, h):
                for t in range(min(4, cut // LANES)):
                    at = pl.ds(pl.multiple_of(k * (4 * LANES) + t * LANES, LANES), LANES)
                    x = raw[blk, h, :, at].astype(jnp.float32)
                    to = pl.ds(pl.multiple_of(h * cut + k * (4 * LANES) + t * LANES, LANES), LANES)
                    scaled[:, to] = (x * gain[:, to]).astype(jnp.bfloat16)
                    sq = sq + x * x
                return sq

            rows = hid.shape[0]
            sq = jnp.zeros((rows, LANES), jnp.float32)
            for h in range(pieces):
                sq = lax.fori_loop(0, max(1, cut // (4 * LANES)), functools.partial(prep, h=h), sq)

            @pl.when(j == 0)
            def _():
                for i in range(parts_kv):
                    kv_weight(i).wait()

            part = jnp.dot(scaled[...], wkv_v[...], preferred_element_type=jnp.float32)
            mine = blk == nar

            @pl.when(mine)
            def _():
                own_s[:, :kv] = part
                own_s[:, kv:] = sq

            @pl.when(jnp.logical_not(mine))
            def _():
                stage_s[blk, :, :kv] = part.astype(jnp.bfloat16)
                coarse = sq.astype(jnp.bfloat16)
                stage_s[blk, :, kv:kv + LANES] = coarse
                stage_s[blk, :, kv + LANES:] = (sq - coarse.astype(jnp.float32)).astype(jnp.bfloat16)
                send_s(blk).start()

            @pl.loop(0, chunks)
            def _(c):
                @pl.when(j == 0)
                def _():
                    q_weight(c).wait()

                piece = jnp.dot(scaled[...], wq_v[c], preferred_element_type=jnp.float32)

                @pl.when(mine)
                def _():
                    own_q[c] = piece

                @pl.when(jnp.logical_not(mine))
                def _():
                    stage_q[blk, c] = piece.astype(jnp.bfloat16)

                @pl.when(blk == buddy)
                def _():
                    send_q(blk, c).start()

                @pl.when((blk // 2 != chip) & (lax.rem(c, 2) != core))
                def _():
                    swap_q(blk, c).start()

                    @pl.when(c > 0)
                    def _():
                        combine(blk, c - 1)

                for h in range(pieces):
                    @pl.when(lead & (c == jnp.where(j == 0, points[0][h], points[1][h])))
                    def _():
                        forward(d + 1, h)

            @pl.when((blk // 2 != chip) & (lax.rem(chunks - 1, 2) == core))
            def _():
                combine(blk, chunks - 1)

    def recv_s(p):
        return pltpu.make_async_remote_copy(
            src_ref=stage_s.at[p], dst_ref=got_s.at[p], send_sem=ss_sem.at[p], recv_sem=rs_sem.at[p],
            device_id={"narrow": p}, device_id_type=MESH_ID)

    def recv_q(p, c):
        return pltpu.make_async_remote_copy(
            src_ref=stage_q.at[p, c], dst_ref=got_q.at[p, c], send_sem=sq_sem.at[p, c], recv_sem=rq_sem.at[p, c],
            device_id={"narrow": p}, device_id_type=MESH_ID)

    for i in range(1, n):
        p = lax.rem(nar + i, n)
        recv_s(p).wait_recv()
        block = got_s[p].astype(jnp.float32)
        own_s[:, :kv] += block[:, :kv]
        own_s[:, kv:] += block[:, kv:kv + LANES] + block[:, kv + LANES:]
    squares = jnp.sum(own_s[:, kv:], axis=1, keepdims=True)
    inverse = lax.rsqrt(squares / D + 1e-05)
    made = []
    for t in range(kv // LANES):
        at = slice(t * LANES, (t + 1) * LANES)
        u = own_s[:, at] * inverse
        if not aligned:
            u = turn(u, tables[0][:, at], tables[1][:, at])
        elif t * LANES < key_cols:
            u = turn(u, cos[...], sin[...])
        made.append(u)
    joint = jnp.concatenate(made, axis=1) if len(made) > 1 else made[0]
    out_k[...] = joint[:, :key_cols].astype(jnp.bfloat16)
    out_v[...] = joint[:, key_cols:].astype(jnp.bfloat16)

    @pl.loop(0, chunks)
    def _(c):
        sources = [buddy]
        for i in range(1, n // 2):
            sources.append(2 * lax.rem(chip + i, n // 2) + lax.rem(c, 2))
        for p in sources:
            recv_q(p, c).wait_recv()
        for t in range(width // LANES):
            at = pl.ds(t * LANES, LANES)
            u = own_q[c, :, at]
            for p in sources:
                u = u + got_q[p, c, :, at].astype(jnp.float32)
            turned = turn(u * inverse, cos[...], sin[...])
            out_q[:, pl.ds(pl.multiple_of(c * width + t * LANES, LANES), LANES)] = turned.astype(jnp.bfloat16)

    @pl.loop(0, n)
    def _(b):
        @pl.when((b <= me) & (me < n - 1))
        def _():
            for h in range(pieces):
                up(b, h).wait_send()

        @pl.when((b >= me) & (me > 0))
        def _():
            for h in range(pieces):
                down(b, h).wait_send()

    for i in range(1, n):
        b = lax.rem(nar + i, n)
        send_s(b).wait_send()

        @pl.loop(0, chunks)
        def _(c):
            send_q(b, c).wait_send()


def hand_over(*refs):
    for i in range(3):
        refs[3 + i][...] = refs[i][...]


def shards(n, hidden_in, norm_gain, query_weight, key_weight, value_weight, positions):
    rows, depth = hidden_in.shape
    query_cols = query_weight.shape[1]
    key_cols = key_weight.shape[1]
    kv = 2 * key_cols
    width = 512
    chunks = query_cols // width
    lanes = jnp.arange(HEAD_DIM, dtype=jnp.int32)
    angle = positions.astype(jnp.float32)[:, None] * frequency((lanes // 2).astype(jnp.float32), HEAD_DIM)[None, :]
    cosine = jnp.cos(angle)
    sine = jnp.where(lanes % 2 == 0, -1.0, 1.0)[None, :] * jnp.sin(angle)
    if key_cols % HEAD_DIM == 0:
        tables = ()
        weights = (key_weight, value_weight)
    else:
        start = lax.axis_index("wide") * key_cols % HEAD_DIM
        key_cos = lax.dynamic_slice_in_dim(cosine, start, key_cols, 1)
        key_sin = lax.dynamic_slice_in_dim(sine, start, key_cols, 1)
        weights = (jnp.concatenate([key_weight, value_weight], axis=1),)
        key_cos = jnp.concatenate([key_cos, jnp.ones_like(key_cos)], axis=1)
        key_sin = jnp.concatenate([key_sin, jnp.zeros_like(key_sin)], axis=1)
        tables = (key_cos, key_sin)
    vmem = pl.BlockSpec(memory_space=pltpu.VMEM)
    hbm = pl.BlockSpec(memory_space=pl.ANY)
    bf, f32 = jnp.bfloat16, jnp.float32
    dma = pltpu.SemaphoreType.DMA
    pieces = 2
    points = tuple(tuple(p * chunks // 8 for p in at) for at in ((2, 6), (3, 7)))
    results = pl.pallas_call(
        functools.partial(kernel, n, len(weights), width, pieces, points, not tables),
        out_shape=(
            jax.ShapeDtypeStruct((rows, query_cols), bf),
            jax.ShapeDtypeStruct((rows, key_cols), bf),
            jax.ShapeDtypeStruct((rows, key_cols), bf),
        ),
        in_specs=[vmem] * (4 + len(tables)) + [hbm] * (1 + len(weights)),
        out_specs=(vmem, vmem, vmem),
        scratch_shapes=[
            pltpu.VMEM((n, pieces, rows, depth // pieces), bf),
            pltpu.VMEM((rows, depth), bf),
            pltpu.VMEM((chunks, depth, width), bf),
            pltpu.VMEM((depth, kv), bf),
            pltpu.VMEM((n, chunks, rows, width), bf),
            pltpu.VMEM((n, rows, kv + 2 * LANES), bf),
            pltpu.VMEM((n, chunks, rows, width), bf),
            pltpu.VMEM((n, chunks, rows, width), bf),
            pltpu.VMEM((n, rows, kv + 2 * LANES), bf),
            pltpu.VMEM((chunks, rows, width), f32),
            pltpu.VMEM((rows, kv + LANES), f32),
            dma((n, pieces)), dma((n, pieces)), dma((n, pieces)),
            dma((chunks,)), dma((len(weights),)),
            dma((n, chunks)), dma((n, chunks)), dma((n,)),
            dma((n, chunks)), dma((n,)),
        ],
        compiler_params=pltpu.CompilerParams(
            collective_id=0, has_side_effects=True, vmem_limit_bytes=58 * 1024 * 1024),
        cost_estimate=pl.CostEstimate(
            flops=2 * n * rows * depth * (query_cols + kv),
            bytes_accessed=2 * depth * (query_cols + kv), transcendentals=0),
    )(hidden_in, norm_gain[None, :], cosine, sine, *tables, query_weight, *weights)
    return pl.pallas_call(
        hand_over,
        out_shape=tuple(jax.ShapeDtypeStruct(x.shape, x.dtype) for x in results),
        in_specs=[vmem] * 3,
        out_specs=(vmem,) * 3,
    )(*results)


def solution(mesh):
    n = mesh.shape["narrow"]
    assert mesh.shape["wide"] == n
    return jax.shard_map(
        functools.partial(shards, n),
        mesh=mesh,
        in_specs=(
            P(("grp", "wide"), "narrow"),
            P("narrow"),
            P("narrow", "wide"),
            P("narrow", "wide"),
            P("narrow", "wide"),
            P(("grp", "narrow")),
        ),
        out_specs=(
            P(("grp", "narrow"), "wide"),
            P(("grp", "narrow"), "wide"),
            P(("grp", "narrow"), "wide"),
        ),
        check_vma=False,
    )
```

```python
import functools
import math

import jax
import jax.numpy as jnp
from jax import lax
from jax.experimental import pallas as pl
from jax.experimental.pallas import tpu as pltpu
from jax.sharding import PartitionSpec as P

D = 16384
HEAD_DIM = 128
LANES = 128
MESH_ID = pl.DeviceIdType.MESH


def frequency(pair_index, head_dim):
    base = jnp.float32(500000.0) ** (-2.0 * pair_index / jnp.float32(head_dim))
    wavelen = 2.0 * math.pi / base
    smooth = (8192.0 / wavelen - 1.0) / 3.0
    middle = (1.0 - smooth) * base / 8.0 + smooth * base
    return jnp.where(wavelen < 2048.0, base, jnp.where(wavelen > 8192.0, base / 8.0, middle))


def turn(u, cosine, sine):
    lane = lax.broadcasted_iota(jnp.int32, u.shape, 1)
    other = jnp.where(lane % 2 == 0, pltpu.roll(u, LANES - 1, 1), pltpu.roll(u, 1, 1))
    return u * cosine + other * sine


def kernel(n, parts_kv, width, pieces, points, aligned, hid, gain, cos, sin, *rest):
    tables = rest[:0 if aligned else 2]
    wq, rest = rest[len(tables)], rest[len(tables) + 1:]
    wkv = rest[:parts_kv]
    (out_q, out_k, out_v, raw, scaled, wq_v, wkv_v, stage_q, stage_s, got_q, pair_q, got_s, own_q, own_s,
     up_sem, down_sem, in_sem, wq_sem, wkv_sem, sq_sem, pq_sem, ss_sem, rq_sem, rs_sem) = rest[parts_kv:]
    me = lax.axis_index("wide")
    nar = lax.axis_index("narrow")
    depth = hid.shape[1]
    chunks = wq_v.shape[0]
    kv = wkv_v.shape[1]
    key_cols = kv // 2

    def q_weight(c):
        return pltpu.make_async_copy(wq.at[:, pl.ds(pl.multiple_of(c * width, width), width)], wq_v.at[c], wq_sem.at[c])

    def kv_weight(i):
        w = kv // parts_kv
        return pltpu.make_async_copy(wkv[i], wkv_v.at[:, pl.ds(i * w, w)], wkv_sem.at[i])

    def up(blk, h):
        return pltpu.make_async_remote_copy(
            src_ref=raw.at[blk, h], dst_ref=raw.at[blk, h], send_sem=up_sem.at[blk, h], recv_sem=in_sem.at[blk, h],
            device_id={"wide": lax.rem(me + 1, n)}, device_id_type=MESH_ID)

    def down(blk, h):
        return pltpu.make_async_remote_copy(
            src_ref=raw.at[blk, h], dst_ref=raw.at[blk, h], send_sem=down_sem.at[blk, h], recv_sem=in_sem.at[blk, h],
            device_id={"wide": lax.rem(me + n - 1, n)}, device_id_type=MESH_ID)

    def send_q(blk, c):
        return pltpu.make_async_remote_copy(
            src_ref=stage_q.at[blk, c], dst_ref=got_q.at[nar, c], send_sem=sq_sem.at[blk, c],
            recv_sem=rq_sem.at[nar, c], device_id={"narrow": blk}, device_id_type=MESH_ID)

    core = lax.rem(nar, 2)
    chip = nar // 2
    buddy = nar + 1 - 2 * core

    def swap_q(blk, c):
        return pltpu.make_async_remote_copy(
            src_ref=stage_q.at[blk, c], dst_ref=pair_q.at[blk, c], send_sem=sq_sem.at[blk, c],
            recv_sem=pq_sem.at[blk, c], device_id={"narrow": buddy}, device_id_type=MESH_ID)

    def combine(blk, c):
        swap_q(blk, c).wait_recv()
        both = stage_q[blk, c].astype(jnp.float32) + pair_q[blk, c].astype(jnp.float32)
        stage_q[blk, c] = both.astype(jnp.bfloat16)
        send_q(blk, c).start()

    def send_s(blk):
        return pltpu.make_async_remote_copy(
            src_ref=stage_s.at[blk], dst_ref=got_s.at[nar], send_sem=ss_sem.at[blk],
            recv_sem=rs_sem.at[nar], device_id={"narrow": blk}, device_id_type=MESH_ID)

    for i in range(parts_kv):
        kv_weight(i).start()

    @pl.loop(0, chunks)
    def _(c):
        q_weight(c).start()

    cut = depth // pieces
    for h in range(pieces):
        raw[me, h] = hid[:, h * cut:(h + 1) * cut]
    barrier = pltpu.get_barrier_semaphore()

    @pl.when(me < n - 1)
    def _():
        pl.semaphore_signal(barrier, inc=1, device_id={"wide": lax.rem(me + 1, n)}, device_id_type=MESH_ID)

    @pl.when(me > 0)
    def _():
        pl.semaphore_signal(barrier, inc=1, device_id={"wide": lax.rem(me + n - 1, n)}, device_id_type=MESH_ID)

    for i in range(1, n):
        pl.semaphore_signal(barrier, inc=1, device_id={"narrow": lax.rem(nar + i, n)}, device_id_type=MESH_ID)
    edge = jnp.where(me > 0, 1, 0) + jnp.where(me < n - 1, 1, 0)
    pl.semaphore_wait(barrier, n - 1 + edge)

    @pl.when(me < n - 1)
    def _():
        for h in range(pieces):
            up(me, h).start()

    @pl.when(me > 0)
    def _():
        for h in range(pieces):
            down(me, h).start()

    def forward(d, h):
        low = me - d
        high = me + d

        @pl.when((low >= 0) & (me < n - 1))
        def _():
            up(low, h).wait_recv()
            up(low, h).start()

        @pl.when((high < n) & (me > 0))
        def _():
            down(high, h).wait_recv()
            down(high, h).start()

    @pl.loop(0, 2 * n - 1)
    def _(j):
        d = (j + 1) // 2
        minus = lax.rem(j, 2) == 1
        blk = jnp.where(minus, me - d, me + d)
        valid = (blk >= 0) & (blk < n)
        lead = minus | (j == 0) | (me - d < 0)

        @pl.when(valid)
        def _():
            last_here = jnp.where(minus, me == n - 1, me == 0)

            @pl.when((j > 0) & last_here)
            def _():
                for h in range(pieces):
                    up(blk, h).wait_recv()

            def prep(k, sq, h):
                for t in range(min(4, cut // LANES)):
                    at = pl.ds(pl.multiple_of(k * (4 * LANES) + t * LANES, LANES), LANES)
                    x = raw[blk, h, :, at].astype(jnp.float32)
                    to = pl.ds(pl.multiple_of(h * cut + k * (4 * LANES) + t * LANES, LANES), LANES)
                    scaled[:, to] = (x * gain[:, to]).astype(jnp.bfloat16)
                    sq = sq + x * x
                return sq

            rows = hid.shape[0]
            sq = jnp.zeros((rows, LANES), jnp.float32)
            for h in range(pieces):
                sq = lax.fori_loop(0, max(1, cut // (4 * LANES)), functools.partial(prep, h=h), sq)

            @pl.when(j == 0)
            def _():
                for i in range(parts_kv):
                    kv_weight(i).wait()

            part = jnp.dot(scaled[...], wkv_v[...], preferred_element_type=jnp.float32)
            mine = blk == nar

            @pl.when(mine)
            def _():
                own_s[:, :kv] = part
                own_s[:, kv:] = sq

            @pl.when(jnp.logical_not(mine))
            def _():
                stage_s[blk, :, :kv] = part.astype(jnp.bfloat16)
                coarse = sq.astype(jnp.bfloat16)
                stage_s[blk, :, kv:kv + LANES] = coarse
                stage_s[blk, :, kv + LANES:] = (sq - coarse.astype(jnp.float32)).astype(jnp.bfloat16)
                send_s(blk).start()

            @pl.loop(0, chunks)
            def _(c):
                @pl.when(j == 0)
                def _():
                    q_weight(c).wait()

                piece = jnp.dot(scaled[...], wq_v[c], preferred_element_type=jnp.float32)

                @pl.when(mine)
                def _():
                    own_q[c] = piece

                @pl.when(jnp.logical_not(mine))
                def _():
                    stage_q[blk, c] = piece.astype(jnp.bfloat16)

                @pl.when(blk == buddy)
                def _():
                    send_q(blk, c).start()

                @pl.when((blk // 2 != chip) & (lax.rem(c, 2) != core))
                def _():
                    swap_q(blk, c).start()

                    @pl.when(c > 0)
                    def _():
                        combine(blk, c - 1)

                for h in range(pieces):
                    @pl.when(lead & (c == jnp.where(j == 0, points[0][h], points[1][h])))
                    def _():
                        forward(d + 1, h)

            @pl.when((blk // 2 != chip) & (lax.rem(chunks - 1, 2) == core))
            def _():
                combine(blk, chunks - 1)

    def recv_s(p):
        return pltpu.make_async_remote_copy(
            src_ref=stage_s.at[p], dst_ref=got_s.at[p], send_sem=ss_sem.at[p], recv_sem=rs_sem.at[p],
            device_id={"narrow": p}, device_id_type=MESH_ID)

    def recv_q(p, c):
        return pltpu.make_async_remote_copy(
            src_ref=stage_q.at[p, c], dst_ref=got_q.at[p, c], send_sem=sq_sem.at[p, c], recv_sem=rq_sem.at[p, c],
            device_id={"narrow": p}, device_id_type=MESH_ID)

    for i in range(1, n):
        p = lax.rem(nar + i, n)
        recv_s(p).wait_recv()
        block = got_s[p].astype(jnp.float32)
        own_s[:, :kv] += block[:, :kv]
        own_s[:, kv:] += block[:, kv:kv + LANES] + block[:, kv + LANES:]
    squares = jnp.sum(own_s[:, kv:], axis=1, keepdims=True)
    inverse = lax.rsqrt(squares / D + 1e-05)
    made = []
    for t in range(kv // LANES):
        at = slice(t * LANES, (t + 1) * LANES)
        u = own_s[:, at] * inverse
        if not aligned:
            u = turn(u, tables[0][:, at], tables[1][:, at])
        elif t * LANES < key_cols:
            u = turn(u, cos[...], sin[...])
        made.append(u)
    joint = jnp.concatenate(made, axis=1) if len(made) > 1 else made[0]
    out_k[...] = joint[:, :key_cols].astype(jnp.bfloat16)
    out_v[...] = joint[:, key_cols:].astype(jnp.bfloat16)

    @pl.loop(0, chunks)
    def _(c):
        sources = [buddy]
        for i in range(1, n // 2):
            sources.append(2 * lax.rem(chip + i, n // 2) + lax.rem(c, 2))
        for p in sources:
            recv_q(p, c).wait_recv()
        for t in range(width // LANES):
            at = pl.ds(t * LANES, LANES)
            u = own_q[c, :, at]
            for p in sources:
                u = u + got_q[p, c, :, at].astype(jnp.float32)
            turned = turn(u * inverse, cos[...], sin[...])
            out_q[:, pl.ds(pl.multiple_of(c * width + t * LANES, LANES), LANES)] = turned.astype(jnp.bfloat16)

    @pl.loop(0, n)
    def _(b):
        @pl.when((b <= me) & (me < n - 1))
        def _():
            for h in range(pieces):
                up(b, h).wait_send()

        @pl.when((b >= me) & (me > 0))
        def _():
            for h in range(pieces):
                down(b, h).wait_send()

    for i in range(1, n):
        b = lax.rem(nar + i, n)
        send_s(b).wait_send()

        @pl.loop(0, chunks)
        def _(c):
            send_q(b, c).wait_send()


def hand_over(*refs):
    for i in range(3):
        refs[3 + i][...] = refs[i][...]


def shards(n, hidden_in, norm_gain, query_weight, key_weight, value_weight, positions):
    rows, depth = hidden_in.shape
    query_cols = query_weight.shape[1]
    key_cols = key_weight.shape[1]
    kv = 2 * key_cols
    width = min(1024, query_cols)
    chunks = query_cols // width
    lanes = jnp.arange(HEAD_DIM, dtype=jnp.int32)
    angle = positions.astype(jnp.float32)[:, None] * frequency((lanes // 2).astype(jnp.float32), HEAD_DIM)[None, :]
    cosine = jnp.cos(angle)
    sine = jnp.where(lanes % 2 == 0, -1.0, 1.0)[None, :] * jnp.sin(angle)
    if key_cols % HEAD_DIM == 0:
        tables = ()
        weights = (key_weight, value_weight)
    else:
        start = lax.axis_index("wide") * key_cols % HEAD_DIM
        key_cos = lax.dynamic_slice_in_dim(cosine, start, key_cols, 1)
        key_sin = lax.dynamic_slice_in_dim(sine, start, key_cols, 1)
        weights = (jnp.concatenate([key_weight, value_weight], axis=1),)
        key_cos = jnp.concatenate([key_cos, jnp.ones_like(key_cos)], axis=1)
        key_sin = jnp.concatenate([key_sin, jnp.zeros_like(key_sin)], axis=1)
        tables = (key_cos, key_sin)
    vmem = pl.BlockSpec(memory_space=pltpu.VMEM)
    hbm = pl.BlockSpec(memory_space=pl.ANY)
    bf, f32 = jnp.bfloat16, jnp.float32
    dma = pltpu.SemaphoreType.DMA
    pieces = 2
    points = tuple(tuple(p * chunks // 8 for p in at) for at in ((2, 6), (3, 7)))
    results = pl.pallas_call(
        functools.partial(kernel, n, len(weights), width, pieces, points, not tables),
        out_shape=(
            jax.ShapeDtypeStruct((rows, query_cols), bf),
            jax.ShapeDtypeStruct((rows, key_cols), bf),
            jax.ShapeDtypeStruct((rows, key_cols), bf),
        ),
        in_specs=[vmem] * (4 + len(tables)) + [hbm] * (1 + len(weights)),
        out_specs=(vmem, vmem, vmem),
        scratch_shapes=[
            pltpu.VMEM((n, pieces, rows, depth // pieces), bf),
            pltpu.VMEM((rows, depth), bf),
            pltpu.VMEM((chunks, depth, width), bf),
            pltpu.VMEM((depth, kv), bf),
            pltpu.VMEM((n, chunks, rows, width), bf),
            pltpu.VMEM((n, rows, kv + 2 * LANES), bf),
            pltpu.VMEM((n, chunks, rows, width), bf),
            pltpu.VMEM((n, chunks, rows, width), bf),
            pltpu.VMEM((n, rows, kv + 2 * LANES), bf),
            pltpu.VMEM((chunks, rows, width), f32),
            pltpu.VMEM((rows, kv + LANES), f32),
            dma((n, pieces)), dma((n, pieces)), dma((n, pieces)),
            dma((chunks,)), dma((len(weights),)),
            dma((n, chunks)), dma((n, chunks)), dma((n,)),
            dma((n, chunks)), dma((n,)),
        ],
        compiler_params=pltpu.CompilerParams(
            collective_id=0, has_side_effects=True, vmem_limit_bytes=58 * 1024 * 1024),
        cost_estimate=pl.CostEstimate(
            flops=2 * n * rows * depth * (query_cols + kv),
            bytes_accessed=2 * depth * (query_cols + kv), transcendentals=0),
    )(hidden_in, norm_gain[None, :], cosine, sine, *tables, query_weight, *weights)
    return pl.pallas_call(
        hand_over,
        out_shape=tuple(jax.ShapeDtypeStruct(x.shape, x.dtype) for x in results),
        in_specs=[vmem] * 3,
        out_specs=(vmem,) * 3,
    )(*results)


def solution(mesh):
    n = mesh.shape["narrow"]
    assert mesh.shape["wide"] == n
    return jax.shard_map(
        functools.partial(shards, n),
        mesh=mesh,
        in_specs=(
            P(("grp", "wide"), "narrow"),
            P("narrow"),
            P("narrow", "wide"),
            P("narrow", "wide"),
            P("narrow", "wide"),
            P(("grp", "narrow")),
        ),
        out_specs=(
            P(("grp", "narrow"), "wide"),
            P(("grp", "narrow"), "wide"),
            P(("grp", "narrow"), "wide"),
        ),
        check_vma=False,
    )
```
